512 devices in a mesh: replica: 16 (over z_hi, x, core), section: 4 (over z_lo), tensor: 8 (over y).
Axes of the slice: x: 4, y: 8, z: 8 (z_hi: 2, z_lo: 4; z = z_hi * 4 + z_lo), core: 2. Of those that a mesh axis runs over, the one named last changes fastest.
Arguments:
- tokens: bfloat16 [16, 2, 256, 2048], P('replica', None, None, 'tensor'), may hold values from -6 to 6
- query_weight: bfloat16 [16, 4, 2048, 1024], P('replica', 'section', None, 'tensor'), may hold values from -5.524272 to 5.524272
- key_weight: bfloat16 [16, 4, 2048, 1024], P('replica', 'section', None, 'tensor'), may hold values from -0.13479223 to 0.13479223
- value_weight: bfloat16 [16, 4, 2048, 1024], P('replica', 'section', None, 'tensor'), may hold values from -0.125 to 0.125
- slow_output: bfloat16 [16, 4, 1024, 2048], P('replica', 'section', None, 'tensor'), may hold values from -0.75 to 0.75
- momentum: bfloat16 [16, 4, 1024, 2048], P('replica', 'section', None, 'tensor'), may hold values from -3 to 3
- out_grad: bfloat16 [16, 4, 2, 256, 2048], P('replica', 'section', None, None, 'tensor'), may hold values from -6 to 6
- route_keys: int32 [3, 2], replicated, may hold values from 0 to 15
- gossip_partner: int32 [4, 16], replicated, may hold values from 0 to 15, as said below
- positions: int32 [16, 2, 256], replicated, may hold values from 0 to 255, as said below
Outputs:
- section_outputs: bfloat16 [16, 4, 2, 256, 2048], P('replica', 'section', None, None, 'tensor')
- new_slow: bfloat16 [16, 4, 1024, 2048], P('replica', 'section', None, 'tensor')
- new_momentum: bfloat16 [16, 4, 1024, 2048], P('replica', 'section', None, 'tensor')
The draws below stay inside these ranges and needn't reach their ends.
Inputs may be any that keep to these rules, and one draw needn't show every extreme that they name: For each section s, gossip_partner[s, r] = r XOR k_s for one k_s of 1 to 15, the same for every r. positions[r, m, 0] = 0, and each next entry is 0 (a new document) or one more than the one before.
All inputs are finite; a program needn't handle non-finite values.
Results may differ from the reference program's by a relative error of at most 0.018.
Values may be sent and summed in bfloat16 or wider, within the bound.
A program may use at most 64 MiB of HBM per device.

```python
import math
import jax
import jax.numpy as jnp
from jax import lax

D = 2048
HD = 128
SEQ = 256
MICRO = 2
HH = 1024
REPLICAS = 16
SECTIONS = 4
N_REPLICA = 16


def key_basis(key):
    return jnp.clip(jax.random.normal(key, (REPLICAS, SECTIONS, D, HH), jnp.float32), -6.0, 6.0)


def draw_key_weight(key, part):
    basis = key_basis(key)
    return (basis * D ** (-0.5)).astype(jnp.bfloat16)


def draw_query_weight(key, part):
    basis = key_basis(key)
    key = jax.random.fold_in(key, 7)
    own_key = jax.random.fold_in(key, 0)
    own_part = jnp.clip(jax.random.normal(own_key, basis.shape, jnp.float32), -6.0, 6.0)
    return (own_part * D ** (-0.5)).astype(jnp.bfloat16)


def draw_tokens(key, part):
    key = jax.random.fold_in(key, 5)
    basis_key = jax.random.fold_in(key, 0)
    basis = jax.random.normal(basis_key, (REPLICAS, MICRO, SEQ, D), jnp.float32)
    return jnp.clip(basis, -6.0, 6.0).astype(jnp.bfloat16)


def draw_gossip_partner(key, part):
    key = jax.random.fold_in(key, 9)
    pair_masks = jax.random.randint(key, (SECTIONS, 1), 1, REPLICAS)
    return jnp.bitwise_xor(jnp.arange(REPLICAS, dtype=jnp.int32)[None, :], pair_masks).astype(jnp.int32)


def draw_positions(key, part):
    key = jax.random.fold_in(key, 11)
    position_ids = jnp.arange(SEQ, dtype=jnp.int32)
    starts_at = jax.random.randint(key, (REPLICAS, MICRO, SEQ), 0, SEQ) < 4
    starts_at = starts_at.at[:, :, 0].set(True)
    starts_at = starts_at.at[0, 0, :].set(position_ids == 0)
    latest = lax.cummax(jnp.where(starts_at, position_ids[None, None, :], 0), axis=2)
    return (position_ids[None, None, :] - latest).astype(jnp.int32)


def place_ends(drawn, rng, smallest, largest):
    index_at = [jax.random.randint(jax.random.fold_in(rng, axis), (), 0, length) for axis, length in enumerate(drawn.shape)]
    widest = drawn.shape.index(max(drawn.shape))
    next_to = index_at[:widest] + [(index_at[widest] + 1) % drawn.shape[widest]] + index_at[widest + 1:]
    return drawn.at[tuple(index_at)].set(smallest).at[tuple(next_to)].set(largest)


def steps_of(rng, shape, cuts, least, high):
    factor_of = 1.0
    for position, shards_of in cuts:
        draws = jax.random.uniform(jax.random.fold_in(jax.random.fold_in(rng, 6), position), (shards_of,), jnp.float32, least / len(cuts), high / len(cuts))
        factor_of = factor_of * jnp.repeat(jnp.exp(draws), shape[position] // shards_of).reshape((-1,) + (1,) * (len(shape) - 1 - position))
    return factor_of


def noise(key, dims, scale, limit, shards=(), kind=jnp.bfloat16):
    values = jax.random.normal(key, dims, jnp.float32) * scale
    if len(shards) > 0:
        values = steps_of(key, dims, shards, -0.22, 0.18) * values
    return jnp.clip(values, min=-limit, max=limit).astype(kind)


def setup_inputs(seed: int = 0) -> dict:
    keys = jax.random.split(jax.random.key(seed), 11)
    return {
        "tokens": draw_tokens(jax.random.fold_in(keys[10], 71), 0),
        "query_weight": draw_query_weight(jax.random.fold_in(keys[10], 71), 0),
        "key_weight": draw_key_weight(jax.random.fold_in(keys[10], 71), 0),
        "value_weight": noise(keys[3], (REPLICAS, SECTIONS, D, HH), D ** -0.5, 0.125, ((0, 16), (1, 4), (3, 8))),
        "slow_output": noise(keys[4], (REPLICAS, SECTIONS, HH, D), (HH // 16) ** -0.5, 0.75, ((0, 16), (1, 4), (3, 8))),
        "momentum": noise(keys[5], (REPLICAS, SECTIONS, HH, D), 0.5, 3.0, ((0, 16), (1, 4), (3, 8))),
        "out_grad": noise(keys[6], (REPLICAS, SECTIONS, MICRO, SEQ, D), 1.0, 6.0, ((0, 16), (1, 4), (4, 8))),
        "route_keys": place_ends(jax.random.randint(keys[7], (SECTIONS - 1, MICRO), 0, N_REPLICA), jax.random.fold_in(keys[7], 1), 0, N_REPLICA - 1).astype(jnp.int32),
        "gossip_partner": draw_gossip_partner(jax.random.fold_in(keys[10], 71), 0),
        "positions": draw_positions(jax.random.fold_in(keys[10], 71), 0),
    }


inner_rate = 2.0
outer_rate = 0.7
outer_beta = 0.9
neg_fill = -1e+30
norm_eps = 1e-05

def normalize(current):
    widened = current.astype(jnp.float32)
    return (widened * lax.rsqrt(lax.optimization_barrier(jnp.mean(widened * widened, axis=-1, keepdims=True)) + norm_eps)).astype(jnp.bfloat16)

def attend(query_rows, key_rows, value_rows, doc_pos):
    length = query_rows.shape[0]
    scores = jnp.einsum('qhd,khd->hqk', query_rows.astype(jnp.float32), key_rows.astype(jnp.float32)) * HD ** (-0.5)
    row_ids = jnp.arange(length, dtype=jnp.int32)[:, None]
    col_ids = jnp.arange(length, dtype=jnp.int32)[None, :]
    allowed = (col_ids <= row_ids) & (row_ids - col_ids <= doc_pos[:, None])
    scores = jnp.where(allowed[None], scores, neg_fill)
    row_max = lax.optimization_barrier(jnp.max(scores, axis=-1, keepdims=True))
    expo = jnp.exp(scores - row_max)
    probability = (expo / lax.optimization_barrier(jnp.sum(expo, axis=-1, keepdims=True))).astype(jnp.bfloat16)
    mixed_rows = jnp.einsum('hqk,khd->qhd', probability.astype(jnp.float32), value_rows.astype(jnp.float32))
    return mixed_rows.reshape(length, -1).astype(jnp.bfloat16)

def layer(current, w_query, w_key, w_value, w_out, doc_pos):
    length = current.shape[0]
    normed = normalize(current)
    query_rows = jnp.dot(normed, w_query, preferred_element_type=jnp.float32).astype(jnp.bfloat16).reshape(length, -1, HD)
    key_rows = jnp.dot(normed, w_key, preferred_element_type=jnp.float32).astype(jnp.bfloat16).reshape(length, -1, HD)
    value_rows = jnp.dot(normed, w_value, preferred_element_type=jnp.float32).astype(jnp.bfloat16).reshape(length, -1, HD)
    heads_out = attend(query_rows, key_rows, value_rows, doc_pos)
    result = (current.astype(jnp.float32) + jnp.dot(heads_out, w_out, preferred_element_type=jnp.float32)).astype(jnp.bfloat16)
    return (result, heads_out)

def reference(tokens, query_weight, key_weight, value_weight, slow_output, momentum, out_grad, route_keys, gossip_partner, positions):
    replica_ids = jnp.arange(REPLICAS, dtype=jnp.int32)
    run_layer = jax.vmap(layer)
    grad_sum = jnp.zeros((REPLICAS, SECTIONS, HH, D), jnp.float32)
    per_micro = []
    for micro_index in range(MICRO):
        current = tokens[:, micro_index]
        anchor = replica_ids
        section_list = []
        for section_index in range(SECTIONS):
            doc_pos = positions[anchor, micro_index]
            result, heads_out = run_layer(current, query_weight[:, section_index], key_weight[:, section_index], value_weight[:, section_index], slow_output[:, section_index], doc_pos)
            section_list.append(result)
            term = jnp.einsum('rth,rtd->rhd', heads_out.astype(jnp.float32), out_grad[:, section_index, micro_index].astype(jnp.float32))
            grad_sum = grad_sum.at[:, section_index].add(term)
            if section_index + 1 < SECTIONS:
                source = jnp.bitwise_xor(replica_ids, route_keys[section_index, micro_index]).astype(jnp.int32)
                current = result[source]
                anchor = anchor[source]
        per_micro.append(jnp.stack(section_list, axis=1))
    section_outputs = jnp.stack(per_micro, axis=2)
    delta_local = (grad_sum * (inner_rate / math.sqrt(MICRO * SEQ))).astype(jnp.bfloat16)
    mate_rows = gossip_partner.T.astype(jnp.int32)
    section_cols = jnp.arange(SECTIONS, dtype=jnp.int32)[None, :]
    mate_delta = delta_local[mate_rows, section_cols]
    mate_momentum = momentum[mate_rows, section_cols]
    mean_delta = 0.5 * (delta_local.astype(jnp.float32) + mate_delta.astype(jnp.float32))
    momentum_next = outer_beta * 0.5 * (momentum.astype(jnp.float32) + mate_momentum.astype(jnp.float32)) + mean_delta
    new_slow = slow_output.astype(jnp.float32) - outer_rate * (outer_beta * momentum_next + mean_delta)
    return (section_outputs, new_slow.astype(jnp.bfloat16), momentum_next.astype(jnp.bfloat16))
```

```python
import functools
import math

import jax
import jax.numpy as jnp
from jax import lax
from jax.experimental import pallas as pl
from jax.experimental.pallas import tpu as pltpu
from jax.sharding import PartitionSpec as P

MESH = pl.DeviceIdType.MESH

HD = 128
CHUNKS = 4
inner_rate = 2.0
outer_rate = 0.7
outer_beta = 0.9
neg_fill = -1e30
norm_eps = 1e-05


def bit_groups(replicas):
    bits = replicas.bit_length() - 1
    first = [0] + ([3] if bits > 3 else [])
    second = [b for b in range(bits) if b not in first]
    return first, second


def spread(index, bits):
    return sum(((index >> i) & 1) << b for i, b in enumerate(bits))


def choose(blocks, mask, bits):
    for b in bits:
        flipped = jnp.bitwise_and(jnp.right_shift(mask, b), 1) == 1
        blocks = [jnp.where(flipped, odd, even) for even, odd in zip(blocks[::2], blocks[1::2])]
    return blocks[0]


def kernel(
    cfg,
    route_ref, gossip_ref, pos_ref, tok_ref, wq_ref, wk_ref, wv_ref, wo_ref, mom_ref, grad_ref,
    out_ref, slow_ref, newm_ref,
    first_buf, second_buf, x_buf, heads_buf, k_buf, v_buf,
    delta_buf, mom_a, mom_b, mom_d, del_a, del_b, del_d,
    s_first, r_first, s_second, r_second, s_x, r_x, s_h, r_h,
    s_ma, r_ma, s_mb, r_mb, s_da, r_da, s_db, r_db,
):
    replicas, sections, tensors, units, chunks, rows = cfg
    micros = units // chunks
    first_bits, second_bits = bit_groups(replicas)
    n_first, n_second = 1 << len(first_bits), 1 << len(second_bits)
    rep, sec, ten = lax.axis_index("replica"), lax.axis_index("section"), lax.axis_index("tensor")
    last = sections - 1

    def flip(mask):
        return jnp.bitwise_xor(rep, mask) if mask else rep

    barrier = pltpu.get_barrier_semaphore()
    greeted = 0
    for mask in range(1, replicas):
        pl.semaphore_signal(barrier, inc=1, device_id=(flip(mask), sec, ten), device_id_type=MESH)
        greeted += 1
    for off in range(1, tensors):
        pl.semaphore_signal(
            barrier, inc=1, device_id=(rep, sec, lax.rem(ten + off, tensors)), device_id_type=MESH
        )
        greeted += 1
    for way in (1, sections - 1):
        for e in range(n_first):
            pl.semaphore_signal(
                barrier,
                inc=1,
                device_id=(flip(spread(e, first_bits)), lax.rem(sec + way, sections), ten),
                device_id_type=MESH,
            )
            greeted += 1

    k_buf[...] = jnp.zeros_like(k_buf)
    v_buf[...] = jnp.zeros_like(v_buf)
    pl.semaphore_wait(barrier, greeted)

    def send(src, dst, s_sem, r_sem, where):
        return pltpu.make_async_remote_copy(
            src_ref=src, dst_ref=dst, send_sem=s_sem, recv_sem=r_sem, device_id=where, device_id_type=MESH
        )

    def await_bytes(ref, sem):
        pltpu.make_async_copy(ref, ref, sem).wait()

    pair = gossip_ref[sec, 0]

    def swap_start(src, a, s_sem, r_sem):
        for c in range(1, replicas):
            send(src.at[c], a.at[c], s_sem, r_sem, (flip(c), sec, ten)).start()
        a[0] = src[0]

    def swap_turn(a, b, d, rs_a, s_sem, r_sem):
        await_bytes(a.at[pl.ds(1, replicas - 1)], rs_a)
        for j in range(replicas):
            block = a[jnp.bitwise_xor(pair, j)]
            if j == 0:
                d[0] = block
            else:
                b[j] = block
                send(b.at[j], d.at[j], s_sem, r_sem, (flip(j), sec, ten)).start()

    swap_start(mom_ref, mom_a, s_ma, r_ma)

    @pl.when(sec != 0)
    def _():
        swap_turn(mom_a, mom_b, mom_d, r_ma, s_mb, r_mb)

    def relay_mask(unit):
        return route_ref[jnp.maximum(sec - 1, 0), unit // chunks]

    def stage_pick(unit):
        await_bytes(first_buf.at[unit], r_first.at[unit])
        second_buf[unit, 0] = choose([first_buf[unit, e] for e in range(n_first)], relay_mask(unit), first_bits)
        for j in range(1, n_second):
            send(
                second_buf.at[unit, 0], second_buf.at[unit, j], s_second.at[unit], r_second.at[unit],
                (flip(spread(j, second_bits)), sec, ten),
            ).start()

    def stage_gather(unit):
        @pl.when(sec == 0)
        def _():
            x_buf[unit, ten] = tok_ref[unit]

        @pl.when(sec != 0)
        def _():
            await_bytes(second_buf.at[unit, pl.ds(1, n_second - 1)], r_second.at[unit])
            x_buf[unit, ten] = choose([second_buf[unit, j] for j in range(n_second)], relay_mask(unit), second_bits)

        for off in [o for d in range(tensors // 2, 0, -1) for o in sorted({d, tensors - d})]:
            send(
                x_buf.at[unit, ten], x_buf.at[unit, ten], s_x.at[unit], r_x.at[unit],
                (rep, sec, lax.rem(ten + off, tensors)),
            ).start()

    def stage_attend(unit):
        micro, chunk = unit // chunks, lax.rem(unit, chunks)
        anchor = rep
        for earlier in range(last):
            anchor = jnp.bitwise_xor(anchor, jnp.where(earlier < sec, route_ref[earlier, micro], 0))
        await_bytes(x_buf.at[unit, pl.ds(0, tensors - 1)], r_x.at[unit])
        width = x_buf.shape[3]
        total = jnp.zeros((rows, 3 * HD), jnp.float32)
        squares = jnp.zeros((rows, width), jnp.float32)
        for b in range(tensors):
            block = x_buf[unit, b]
            deep = pl.ds(b * width, width)
            weight = jnp.concatenate([wq_ref[deep, :], wk_ref[deep, :], wv_ref[deep, :]], axis=1)
            total += jnp.dot(block, weight, preferred_element_type=jnp.float32)
            wide = block.astype(jnp.float32)
            squares += wide * wide
        mean = jnp.sum(squares, axis=1, keepdims=True) * (1.0 / (width * tensors))
        qkv = (total * lax.rsqrt(mean + norm_eps)).astype(jnp.bfloat16)
        k_buf[micro, chunk] = qkv[:, HD : 2 * HD]
        v_buf[micro, chunk] = qkv[:, 2 * HD :]
        length = chunks * rows
        keys = k_buf[micro].reshape(length, HD)
        values = v_buf[micro].reshape(length, HD)
        scores = lax.dot_general(
            qkv[:, :HD], keys, (((1,), (1,)), ((), ())), preferred_element_type=jnp.float32
        ) * HD ** (-0.5)
        row_ids = lax.broadcasted_iota(jnp.int32, (rows, length), 0) + chunk * rows
        col_ids = lax.broadcasted_iota(jnp.int32, (rows, length), 1)
        here = pos_ref[anchor, pl.ds(micro, 1), :]
        doc_pos = jnp.sum(
            jnp.where(row_ids == col_ids, jnp.broadcast_to(here, (rows, length)), 0), axis=1, keepdims=True
        )
        allowed = (col_ids <= row_ids) & (row_ids - col_ids <= doc_pos)
        scores = jnp.where(allowed, scores, neg_fill)
        expo = jnp.exp(scores - jnp.max(scores, axis=1, keepdims=True))
        probability = (expo / jnp.sum(expo, axis=1, keepdims=True)).astype(jnp.bfloat16)
        heads = jnp.dot(probability, values, preferred_element_type=jnp.float32)
        heads_buf[unit, ten] = heads.astype(jnp.bfloat16)
        for off in [o for d in range(tensors // 2, 0, -1) for o in sorted({d, tensors - d})]:
            send(
                heads_buf.at[unit, ten], heads_buf.at[unit, ten], s_h.at[unit], r_h.at[unit],
                (rep, sec, lax.rem(ten + off, tensors)),
            ).start()

    def stage_out(unit):
        await_bytes(heads_buf.at[unit, pl.ds(0, tensors - 1)], r_h.at[unit])
        total = x_buf[unit, ten].astype(jnp.float32)
        for b in range(0, tensors, 2):
            both = jnp.concatenate([heads_buf[unit, b], heads_buf[unit, b + 1]], axis=1)
            total += jnp.dot(both, wo_ref[pl.ds(b * HD, 2 * HD), :], preferred_element_type=jnp.float32)
        out_ref[unit] = total.astype(jnp.bfloat16)

        @pl.when(sec != last)
        def _():
            for e in range(n_first - 1, -1, -1):
                send(
                    out_ref.at[unit], first_buf.at[unit, e], s_first.at[unit], r_first.at[unit],
                    (flip(spread(e, first_bits)), lax.rem(sec + 1, sections), ten),
                ).start()

    def tick(t, carry):
        @pl.when((sec != 0) & (t < units))
        def _():
            stage_pick(t)

        @pl.when((t >= 2) & (t < units + 2))
        def _():
            stage_attend(t - 2)

        @pl.when(t < units)
        def _():
            stage_gather(t)

        @pl.when(t >= 3)
        def _():
            stage_out(t - 3)

        return carry

    lax.fori_loop(0, units + 3, tick, 0)

    piece = delta_buf.shape[1]
    per_head = HD // piece if piece <= HD else 1
    scale = inner_rate / math.sqrt(units * rows)

    def delta_step(h, carry):
        mine = heads_buf[:, h].reshape(units * rows, HD)
        grad = lax.dot_general(
            mine, grad_ref[...], (((0,), (0,)), ((), ())), preferred_element_type=jnp.float32
        )
        delta = (grad * scale).astype(jnp.bfloat16)
        for q in range(per_head):
            delta_buf[h * per_head + q] = delta[q * piece : (q + 1) * piece]
        return carry

    lax.fori_loop(0, tensors, delta_step, 0)
    swap_start(delta_buf, del_a, s_da, r_da)

    @pl.when(sec == 0)
    def _():
        swap_turn(mom_a, mom_b, mom_d, r_ma, s_mb, r_mb)

    swap_turn(del_a, del_b, del_d, r_da, s_db, r_db)
    await_bytes(mom_d.at[pl.ds(1, replicas - 1)], r_mb)
    await_bytes(del_d.at[pl.ds(1, replicas - 1)], r_db)

    def update(c, carry):
        there = jnp.bitwise_xor(pair, c)
        mean_delta = 0.5 * (delta_buf[c].astype(jnp.float32) + del_d[there].astype(jnp.float32))
        both = mom_ref[c].astype(jnp.float32) + mom_d[there].astype(jnp.float32)
        momentum_next = outer_beta * 0.5 * both + mean_delta
        old = wo_ref[pl.ds(pl.multiple_of(c * piece, piece), piece), :].astype(jnp.float32)
        slow_ref[c] = (old - outer_rate * (outer_beta * momentum_next + mean_delta)).astype(jnp.bfloat16)
        newm_ref[c] = momentum_next.astype(jnp.bfloat16)
        return carry

    lax.fori_loop(0, replicas, update, 0)

    await_bytes(mom_a.at[pl.ds(1, replicas - 1)], s_ma)
    await_bytes(mom_a.at[pl.ds(1, replicas - 1)], s_mb)
    await_bytes(mom_a.at[pl.ds(1, replicas - 1)], s_da)
    await_bytes(mom_a.at[pl.ds(1, replicas - 1)], s_db)

    def drain(u, carry):
        await_bytes(x_buf.at[u, pl.ds(0, tensors - 1)], s_x.at[u])
        await_bytes(heads_buf.at[u, pl.ds(0, tensors - 1)], s_h.at[u])

        @pl.when(sec != 0)
        def _():
            await_bytes(second_buf.at[u, pl.ds(1, n_second - 1)], s_second.at[u])

        @pl.when(sec != last)
        def _():
            await_bytes(first_buf.at[u], s_first.at[u])

        return carry

    lax.fori_loop(0, units, drain, 0)


def shards(sizes, tokens, query_weight, key_weight, value_weight, slow_output, momentum, out_grad, route_keys,
           gossip_partner, positions):
    replicas, sections, tensors = sizes
    _, micros, length, width = tokens.shape
    chunks = CHUNKS
    rows = length // chunks
    units = micros * chunks
    wo = slow_output[0, 0]
    high = wo.shape[0]
    piece = high // replicas
    first_bits, second_bits = bit_groups(replicas)
    n_first, n_second = 1 << len(first_bits), 1 << len(second_bits)
    bf = jnp.bfloat16
    swap = pltpu.VMEM((replicas, piece, width), bf)
    dma = pltpu.SemaphoreType.DMA
    vmem = pl.BlockSpec(memory_space=pltpu.VMEM)
    smem = pl.BlockSpec(memory_space=pltpu.SMEM)
    cfg = (replicas, sections, tensors, units, chunks, rows)
    out, slow, newm = pl.pallas_call(
        functools.partial(kernel, cfg),
        out_shape=(
            jax.ShapeDtypeStruct((units, rows, width), bf),
            jax.ShapeDtypeStruct((replicas, piece, width), bf),
            jax.ShapeDtypeStruct((replicas, piece, width), bf),
        ),
        in_specs=[smem, smem] + [vmem] * 8,
        out_specs=(vmem, vmem, vmem),
        scratch_shapes=[
            pltpu.VMEM((units, n_first, rows, width), bf),
            pltpu.VMEM((units, n_second, rows, width), bf),
            pltpu.VMEM((units, tensors, rows, width), bf),
            pltpu.VMEM((units, tensors, rows, HD), bf),
            pltpu.VMEM((micros, chunks, rows, HD), bf),
            pltpu.VMEM((micros, chunks, rows, HD), bf),
            swap, swap, swap, swap, swap, swap, swap,
        ]
        + [dma((units,))] * 8
        + [dma] * 8,
        compiler_params=pltpu.CompilerParams(
            collective_id=0, has_side_effects=True, vmem_limit_bytes=40 * 1024 * 1024
        ),
    )(
        route_keys, gossip_partner, positions, tokens.reshape(units, rows, width),
        query_weight[0, 0], key_weight[0, 0], value_weight[0, 0], wo,
        momentum.reshape(replicas, piece, width), out_grad.reshape(units * rows, width),
    )
    return (
        out.reshape(1, 1, micros, length, width),
        slow.reshape(1, 1, high, width),
        newm.reshape(1, 1, high, width),
    )


def solution(mesh):
    sizes = tuple(mesh.shape[a] for a in ("replica", "section", "tensor"))
    weights = P("replica", "section", None, "tensor")
    return jax.shard_map(
        functools.partial(shards, sizes),
        mesh=mesh,
        in_specs=(
            P("replica", None, None, "tensor"),
            weights, weights, weights, weights, weights,
            P("replica", "section", None, None, "tensor"),
            P(), P(), P(),
        ),
        out_specs=(P("replica", "section", None, None, "tensor"), weights, weights),
        check_vma=False,
    )
```

```python
import functools
import math

import jax
import jax.numpy as jnp
from jax import lax
from jax.experimental import pallas as pl
from jax.experimental.pallas import tpu as pltpu
from jax.sharding import PartitionSpec as P

MESH = pl.DeviceIdType.MESH

HD = 128
CHUNKS = 8
PARTS = 2
SCHEDULE = (("pick", 0), ("hand_x", 3), ("hand_heads", 6), ("gather", 1), ("attend", 4), ("out", 7))
inner_rate = 2.0
outer_rate = 0.7
outer_beta = 0.9
neg_fill = -1e30
norm_eps = 1e-05


def bit_groups(replicas):
    bits = replicas.bit_length() - 1
    first = [0] + ([3] if bits > 3 else [])
    second = [b for b in range(bits) if b not in first]
    return first, second


def spread(index, bits):
    return sum(((index >> i) & 1) << b for i, b in enumerate(bits))


def choose(blocks, mask, bits):
    for b in bits:
        flipped = jnp.bitwise_and(jnp.right_shift(mask, b), 1) == 1
        blocks = [jnp.where(flipped, odd, even) for even, odd in zip(blocks[::2], blocks[1::2])]
    return blocks[0]


def kernel(
    cfg,
    route_ref, gossip_ref, pos_in, tok_in, wq_in, wk_in, wv_in, wo_in, mom_in, grad_in,
    out_ref, slow_ref, newm_ref,
    pos_ref, tok_ref, w_ref, wo_ref, mom_ref, grad_ref, grad_acc,
    first_buf, second_buf, x_buf, heads_buf, k_buf, v_buf,
    delta_buf, mom_b, mom_d, del_b, del_d, landed,
    s_first, r_first, s_second, r_second, s_x, r_x, s_h, r_h,
    s_ma, r_ma, s_mb, r_mb, s_da, r_da, s_db, r_db, s_in,
):
    replicas, sections, tensors, units, chunks, rows = cfg
    mom_a, del_a = landed[:PARTS], landed[PARTS:]
    first_bits, second_bits = bit_groups(replicas)
    n_first, n_second = 1 << len(first_bits), 1 << len(second_bits)
    rep, sec, ten = lax.axis_index("replica"), lax.axis_index("section"), lax.axis_index("tensor")
    last = sections - 1

    def flip(mask):
        return jnp.bitwise_xor(rep, mask) if mask else rep

    loads = [
        pltpu.make_async_copy(src, dst, s_in.at[i])
        for i, (src, dst) in enumerate(
            (
                (tok_in, tok_ref),
                (pos_in, pos_ref),
                (wq_in, w_ref.at[:, pl.ds(0, HD)]),
                (wk_in, w_ref.at[:, pl.ds(HD, HD)]),
                (wv_in, w_ref.at[:, pl.ds(2 * HD, HD)]),
                (wo_in, wo_ref),
                (mom_in, mom_ref),
                (grad_in, grad_ref),
            )
        )
    ]
    for load in loads:
        load.start()

    barrier = pltpu.get_barrier_semaphore()
    greeted = 0
    for mask in range(1, replicas):
        pl.semaphore_signal(barrier, inc=1, device_id=(flip(mask), sec, ten), device_id_type=MESH)
        greeted += 1
    for off in range(1, tensors):
        pl.semaphore_signal(
            barrier, inc=1, device_id=(rep, sec, lax.rem(ten + off, tensors)), device_id_type=MESH
        )
        greeted += 1
    for way in (1, sections - 1):
        for e in range(n_first):
            pl.semaphore_signal(
                barrier,
                inc=1,
                device_id=(flip(spread(e, first_bits)), lax.rem(sec + way, sections), ten),
                device_id_type=MESH,
            )
            greeted += 1

    k_buf[...] = jnp.zeros_like(k_buf)
    v_buf[...] = jnp.zeros_like(v_buf)
    for load in loads:
        load.wait()
    pl.semaphore_wait(barrier, greeted)

    def send(src, dst, s_sem, r_sem, where):
        return pltpu.make_async_remote_copy(
            src_ref=src, dst_ref=dst, send_sem=s_sem, recv_sem=r_sem, device_id=where, device_id_type=MESH
        )

    def await_bytes(ref, sem):
        pltpu.make_async_copy(ref, ref, sem).wait()

    pair = gossip_ref[sec, 0]

    part = mom_ref.shape[1] // PARTS
    outward = sorted(range(1, replicas), key=lambda c: (-(c >> 3), -((c >> 1) & 3 == 2), -(c >> 1)))

    def rows_of(p):
        return pl.ds(p * part, part)

    def swap_start(src, a, s_sem, r_sem):
        for p in range(PARTS):
            for c in outward:
                send(
                    src.at[c, rows_of(p)], a[p].at[c], s_sem.at[p], r_sem.at[p], (flip(c), sec, ten)
                ).start()
            a[p][0] = src[0, rows_of(p)]

    def swap_turn(a, b, d, rs_a, s_sem, r_sem):
        for p in range(PARTS):
            await_bytes(a[p].at[pl.ds(1, replicas - 1)], rs_a.at[p])
            for j in outward:
                b[j, rows_of(p)] = a[p][jnp.bitwise_xor(pair, j)]
                send(b.at[j, rows_of(p)], d.at[j, rows_of(p)], s_sem.at[p], r_sem.at[p], (flip(j), sec, ten)).start()
            d[0, rows_of(p)] = a[p][pair]

    def await_part(a, p, sem):
        await_bytes(a.at[pl.ds(1, replicas - 1), rows_of(p)], sem.at[p])

    swap_start(mom_ref, mom_a, s_ma, r_ma)

    @pl.when(sec != 0)
    def _():
        swap_turn(mom_a, mom_b, mom_d, r_ma, s_mb, r_mb)

    def relay_mask(unit):
        return route_ref[jnp.maximum(sec - 1, 0), unit // chunks]

    def beside(off):
        return lax.rem(ten + off + tensors, tensors)

    def near_and_far(buf, unit, s_sem, r_sem):
        for kind, offs in ((1, (2, -2)), (0, (1, -1))):
            for off in offs:
                send(
                    buf.at[unit, ten], buf.at[unit, ten], s_sem.at[unit, kind], r_sem.at[unit, kind],
                    (rep, sec, beside(off)),
                ).start()

    def hand_on(buf, unit, s_sem, r_sem):
        await_bytes(buf.at[unit, pl.ds(0, 2)], r_sem.at[unit, 1])
        for way in (1, -1):
            block = buf.at[unit, beside(-2 * way)]
            half = block.at[pl.ds(0 if way == 1 else rows // 2, rows // 2)]
            for src, off in ((half, 2 * way), (block, way)):
                send(src, src, s_sem.at[unit, 2], r_sem.at[unit, 2], (rep, sec, beside(off))).start()

    def await_rest(buf, unit, r_sem):
        await_bytes(buf.at[unit, pl.ds(0, 2)], r_sem.at[unit, 0])
        await_bytes(buf.at[unit, pl.ds(0, 3)], r_sem.at[unit, 2])

    def stage_pick(unit):
        await_bytes(first_buf.at[unit], r_first.at[unit])
        second_buf[unit, 0] = choose([first_buf[unit, e] for e in range(n_first)], relay_mask(unit), first_bits)
        for j in range(1, n_second):
            send(
                second_buf.at[unit, 0], second_buf.at[unit, j], s_second.at[unit], r_second.at[unit],
                (flip(spread(j, second_bits)), sec, ten),
            ).start()

    def stage_gather(unit):
        @pl.when(sec == 0)
        def _():
            x_buf[unit, ten] = tok_ref[unit]

        @pl.when(sec != 0)
        def _():
            await_bytes(second_buf.at[unit, pl.ds(1, n_second - 1)], r_second.at[unit])
            x_buf[unit, ten] = choose([second_buf[unit, j] for j in range(n_second)], relay_mask(unit), second_bits)

        near_and_far(x_buf, unit, s_x, r_x)

    def stage_hand_x(unit):
        hand_on(x_buf, unit, s_x, r_x)

    def stage_hand_heads(unit):
        hand_on(heads_buf, unit, s_h, r_h)

    def stage_attend(unit):
        micro, chunk = unit // chunks, lax.rem(unit, chunks)
        anchor = rep
        for earlier in range(last):
            anchor = jnp.bitwise_xor(anchor, jnp.where(earlier < sec, route_ref[earlier, micro], 0))
        await_rest(x_buf, unit, r_x)
        width = x_buf.shape[3]
        total = jnp.zeros((rows, 3 * HD), jnp.float32)
        squares = jnp.zeros((rows, width), jnp.float32)
        for b in range(tensors):
            block = x_buf[unit, b]
            deep = pl.ds(b * width, width)
            total += jnp.dot(block, w_ref[deep, :], preferred_element_type=jnp.float32)
            wide = block.astype(jnp.float32)
            squares += wide * wide
        mean = jnp.sum(squares, axis=1, keepdims=True) * (1.0 / (width * tensors))
        qkv = (total * lax.rsqrt(mean + norm_eps)).astype(jnp.bfloat16)
        k_buf[micro, chunk] = qkv[:, HD : 2 * HD]
        v_buf[micro, chunk] = qkv[:, 2 * HD :]
        length = chunks * rows
        keys = k_buf[micro].reshape(length, HD)
        values = v_buf[micro].reshape(length, HD)
        scores = lax.dot_general(
            qkv[:, :HD], keys, (((1,), (1,)), ((), ())), preferred_element_type=jnp.float32
        ) * HD ** (-0.5)
        row_ids = lax.broadcasted_iota(jnp.int32, (rows, length), 0) + chunk * rows
        col_ids = lax.broadcasted_iota(jnp.int32, (rows, length), 1)
        here = pos_ref[anchor, pl.ds(micro, 1), :]
        doc_pos = jnp.sum(
            jnp.where(row_ids == col_ids, jnp.broadcast_to(here, (rows, length)), 0), axis=1, keepdims=True
        )
        allowed = (col_ids <= row_ids) & (row_ids - col_ids <= doc_pos)
        scores = jnp.where(allowed, scores, neg_fill)
        expo = jnp.exp(scores - jnp.max(scores, axis=1, keepdims=True))
        probability = (expo / jnp.sum(expo, axis=1, keepdims=True)).astype(jnp.bfloat16)
        heads = jnp.dot(probability, values, preferred_element_type=jnp.float32)
        heads_buf[unit, ten] = heads.astype(jnp.bfloat16)
        near_and_far(heads_buf, unit, s_h, r_h)

    def stage_out(unit):
        await_rest(heads_buf, unit, r_h)
        total = x_buf[unit, ten].astype(jnp.float32)
        for b in range(0, tensors, 2):
            both = jnp.concatenate([heads_buf[unit, b], heads_buf[unit, b + 1]], axis=1)
            total += jnp.dot(both, wo_ref[pl.ds(b * HD, 2 * HD), :], preferred_element_type=jnp.float32)
        out_ref[unit] = total.astype(jnp.bfloat16)

        @pl.when(sec != last)
        def _():
            for e in range(n_first - 1, -1, -1):
                send(
                    out_ref.at[unit], first_buf.at[unit, e], s_first.at[unit], r_first.at[unit],
                    (flip(spread(e, first_bits)), lax.rem(sec + 1, sections), ten),
                ).start()

    stages = {
        "pick": stage_pick, "gather": stage_gather, "hand_x": stage_hand_x,
        "attend": stage_attend, "hand_heads": stage_hand_heads, "out": stage_out,
    }

    piece = delta_buf.shape[1]
    per_head = HD // piece if piece <= HD else 1
    scale = inner_rate / math.sqrt(units * rows)
    early = (0, units // 2, units - max(1, units // 8))

    def add_up(start, stop, fresh, finish):
        def head(h, carry):
            count = stop - start
            mine = heads_buf[pl.ds(start, count), h].reshape(count * rows, HD)
            grad = lax.dot_general(
                mine, grad_ref[pl.ds(start * rows, count * rows), :], (((0,), (0,)), ((), ())),
                preferred_element_type=jnp.float32,
            )
            if not fresh:
                grad = grad + grad_acc[h]
            if finish:
                delta = (grad * scale).astype(jnp.bfloat16)
                for q in range(per_head):
                    delta_buf[h * per_head + q] = delta[q * piece : (q + 1) * piece]
            else:
                grad_acc[h] = grad
            return carry

        lax.fori_loop(0, tensors, head, 0)

    def tick(t, carry):
        for name, late in SCHEDULE:
            unit = t - late
            due = (unit >= 0) & (unit < units)
            if name == "pick":
                due = due & (sec != 0)
            pl.when(due)(functools.partial(stages[name], unit))

        @pl.when((sec == 0) & (t == units // 2))
        def _():
            swap_turn(mom_a, mom_b, mom_d, r_ma, s_mb, r_mb)

        done = t - dict(SCHEDULE)['out'] + 1
        for start, stop in zip(early, early[1:]):
            pl.when((sec == last) & (done == stop))(functools.partial(add_up, start, stop, start == 0, False))
        return carry

    lax.fori_loop(0, units + max(late for _, late in SCHEDULE), tick, 0)

    @pl.when(sec == last)
    def _():
        add_up(early[-1], units, False, True)

    @pl.when(sec != last)
    def _():
        add_up(0, units, True, True)

    swap_start(delta_buf, del_a, s_da, r_da)

    swap_turn(del_a, del_b, del_d, r_da, s_db, r_db)
    for p in range(PARTS):
        await_part(mom_d, p, r_mb)

    def update(p, c):
        span = rows_of(p)
        there = jnp.bitwise_xor(pair, c)
        mean_delta = 0.5 * (delta_buf[c, span].astype(jnp.float32) + del_d[there, span].astype(jnp.float32))
        both = mom_ref[c, span].astype(jnp.float32) + mom_d[there, span].astype(jnp.float32)
        momentum_next = outer_beta * 0.5 * both + mean_delta
        old = wo_ref[pl.ds(pl.multiple_of(c * piece + p * part, part), part), :].astype(jnp.float32)
        slow_ref[c, span] = (old - outer_rate * (outer_beta * momentum_next + mean_delta)).astype(jnp.bfloat16)
        newm_ref[c, span] = momentum_next.astype(jnp.bfloat16)

    for p in range(PARTS):
        await_part(del_d, p, r_db)

    def update_all(c, carry):
        for p in range(PARTS):
            update(p, c)
        return carry

    lax.fori_loop(0, replicas, update_all, 0)

    for p in range(PARTS):
        await_part(mom_d, p, s_ma)
    for p in range(PARTS):
        await_part(mom_d, p, s_mb)
    for p in range(PARTS):
        await_part(mom_d, p, s_da)
    for p in range(PARTS):
        await_part(mom_d, p, s_db)

    def drain(u, carry):
        for kind, blocks in ((0, 2), (1, 2), (2, 3)):
            await_bytes(x_buf.at[u, pl.ds(0, blocks)], s_x.at[u, kind])
            await_bytes(heads_buf.at[u, pl.ds(0, blocks)], s_h.at[u, kind])

        @pl.when(sec != 0)
        def _():
            await_bytes(second_buf.at[u, pl.ds(1, n_second - 1)], s_second.at[u])

        @pl.when(sec != last)
        def _():
            await_bytes(first_buf.at[u], s_first.at[u])

        return carry

    lax.fori_loop(0, units, drain, 0)


def shards(sizes, tokens, query_weight, key_weight, value_weight, slow_output, momentum, out_grad, route_keys,
           gossip_partner, positions):
    replicas, sections, tensors = sizes
    _, micros, length, width = tokens.shape
    chunks = CHUNKS
    rows = length // chunks
    units = micros * chunks
    wo = slow_output[0, 0]
    high = wo.shape[0]
    piece = high // replicas
    first_bits, second_bits = bit_groups(replicas)
    n_first, n_second = 1 << len(first_bits), 1 << len(second_bits)
    bf = jnp.bfloat16
    swap = pltpu.VMEM((replicas, piece, width), bf)
    dma = pltpu.SemaphoreType.DMA
    vmem = pl.BlockSpec(memory_space=pltpu.VMEM)
    smem = pl.BlockSpec(memory_space=pltpu.SMEM)
    hbm = pl.BlockSpec(memory_space=pl.ANY)
    cfg = (replicas, sections, tensors, units, chunks, rows)
    out, slow, newm = pl.pallas_call(
        functools.partial(kernel, cfg),
        out_shape=(
            jax.ShapeDtypeStruct((units, rows, width), bf),
            jax.ShapeDtypeStruct((replicas, piece, width), bf),
            jax.ShapeDtypeStruct((replicas, piece, width), bf),
        ),
        in_specs=[smem, smem] + [hbm] * 8,
        out_specs=(vmem, vmem, vmem),
        scratch_shapes=[
            pltpu.VMEM(positions.shape, jnp.int32),
            pltpu.VMEM((units, rows, width), bf),
            pltpu.VMEM((width * tensors, 3 * HD), bf),
            pltpu.VMEM(wo.shape, bf),
            swap,
            pltpu.VMEM((units * rows, width), bf),
            pltpu.VMEM((tensors, HD, width), jnp.float32),
            pltpu.VMEM((units, n_first, rows, width), bf),
            pltpu.VMEM((units, n_second, rows, width), bf),
            pltpu.VMEM((units, tensors, rows, width), bf),
            pltpu.VMEM((units, tensors, rows, HD), bf),
            pltpu.VMEM((micros, chunks, rows, HD), bf),
            pltpu.VMEM((micros, chunks, rows, HD), bf),
            swap, swap, swap, swap, swap,
            [pltpu.VMEM((replicas, piece // PARTS, width), bf)] * (2 * PARTS),
        ]
        + [dma((units,))] * 4
        + [dma((units, 3))] * 4
        + [dma((PARTS,))] * 8
        + [dma((8,))],
        compiler_params=pltpu.CompilerParams(
            collective_id=0, has_side_effects=True, vmem_limit_bytes=58 * 1024 * 1024
        ),
    )(
        route_keys, gossip_partner, positions, tokens.reshape(units, rows, width),
        query_weight[0, 0], key_weight[0, 0], value_weight[0, 0], wo,
        momentum.reshape(replicas, piece, width), out_grad.reshape(units * rows, width),
    )
    return (
        out.reshape(1, 1, micros, length, width),
        slow.reshape(1, 1, high, width),
        newm.reshape(1, 1, high, width),
    )


def solution(mesh):
    sizes = tuple(mesh.shape[a] for a in ("replica", "section", "tensor"))
    weights = P("replica", "section", None, "tensor")
    return jax.shard_map(
        functools.partial(shards, sizes),
        mesh=mesh,
        in_specs=(
            P("replica", None, None, "tensor"),
            weights, weights, weights, weights, weights,
            P("replica", "section", None, None, "tensor"),
            P(), P(), P(),
        ),
        out_specs=(P("replica", "section", None, None, "tensor"), weights, weights),
        check_vma=False,
    )
```

```python
import functools
import math

import jax
import jax.numpy as jnp
from jax import lax
from jax.experimental import pallas as pl
from jax.experimental.pallas import tpu as pltpu
from jax.sharding import PartitionSpec as P

MESH = pl.DeviceIdType.MESH

HD = 128
CHUNKS = 8
PARTS = 2
SCHEDULE = (("pick", 0), ("hand_x", 3), ("hand_heads", 6), ("gather", 1), ("attend", 4), ("out", 7))
inner_rate = 2.0
outer_rate = 0.7
outer_beta = 0.9
neg_fill = -1e30
norm_eps = 1e-05


def bit_groups(replicas):
    bits = replicas.bit_length() - 1
    first = [0] + ([3] if bits > 3 else [])
    second = [b for b in range(bits) if b not in first]
    return first, second


def spread(index, bits):
    return sum(((index >> i) & 1) << b for i, b in enumerate(bits))


def choose(blocks, mask, bits):
    for b in bits:
        flipped = jnp.bitwise_and(jnp.right_shift(mask, b), 1) == 1
        blocks = [jnp.where(flipped, odd, even) for even, odd in zip(blocks[::2], blocks[1::2])]
    return blocks[0]


def kernel(
    cfg,
    route_ref, gossip_ref, pos_in, tok_in, wq_in, wk_in, wv_in, wo_in, mom_in, grad_in,
    out_ref, slow_ref, newm_ref,
    pos_ref, tok_ref, w_ref, wo_ref, mom_ref, grad_ref, grad_acc,
    first_buf, second_buf, x_buf, heads_buf, k_buf, v_buf,
    delta_buf, mom_b, mom_d, del_b, del_d, landed,
    s_first, r_first, s_second, r_second, s_x, r_x, s_h, r_h,
    s_ma, r_ma, s_mb, r_mb, s_da, r_da, s_db, r_db, s_in, go,
):
    replicas, sections, tensors, units, chunks, rows = cfg
    mom_a, del_a = landed[:PARTS], landed[PARTS:]
    first_bits, second_bits = bit_groups(replicas)
    n_first, n_second = 1 << len(first_bits), 1 << len(second_bits)
    rep, sec, ten = lax.axis_index("replica"), lax.axis_index("section"), lax.axis_index("tensor")
    last = sections - 1

    def flip(mask):
        return jnp.bitwise_xor(rep, mask) if mask else rep

    loads = [
        pltpu.make_async_copy(src, dst, s_in.at[i])
        for i, (src, dst) in enumerate(
            (
                (tok_in, tok_ref),
                (pos_in, pos_ref),
                (wq_in, w_ref.at[:, pl.ds(0, HD)]),
                (wk_in, w_ref.at[:, pl.ds(HD, HD)]),
                (wv_in, w_ref.at[:, pl.ds(2 * HD, HD)]),
                (wo_in, wo_ref),
                (mom_in, mom_ref),
                (grad_in, grad_ref),
            )
        )
    ]
    for load in loads:
        load.start()

    barrier = pltpu.get_barrier_semaphore()
    greeted = 0
    for mask in range(1, replicas):
        pl.semaphore_signal(barrier, inc=1, device_id=(flip(mask), sec, ten), device_id_type=MESH)
        greeted += 1
    for off in range(1, tensors):
        pl.semaphore_signal(
            barrier, inc=1, device_id=(rep, sec, lax.rem(ten + off, tensors)), device_id_type=MESH
        )
        greeted += 1
    for way in (1, sections - 1):
        for e in range(n_first):
            pl.semaphore_signal(
                barrier,
                inc=1,
                device_id=(flip(spread(e, first_bits)), lax.rem(sec + way, sections), ten),
                device_id_type=MESH,
            )
            greeted += 1

    k_buf[...] = jnp.zeros_like(k_buf)
    v_buf[...] = jnp.zeros_like(v_buf)
    for load in loads:
        load.wait()
    pl.semaphore_wait(barrier, greeted)

    def send(src, dst, s_sem, r_sem, where):
        return pltpu.make_async_remote_copy(
            src_ref=src, dst_ref=dst, send_sem=s_sem, recv_sem=r_sem, device_id=where, device_id_type=MESH
        )

    def await_bytes(ref, sem):
        pltpu.make_async_copy(ref, ref, sem).wait()

    pair = gossip_ref[sec, 0]

    part = mom_ref.shape[1] // PARTS
    outward = sorted(range(1, replicas), key=lambda c: (-(c >> 3), -((c >> 1) & 3 == 2), -(c >> 1)))

    def rows_of(p):
        return pl.ds(p * part, part)

    def swap_start(src, a, s_sem, r_sem):
        for p in range(PARTS):
            for c in outward:
                send(
                    src.at[c, rows_of(p)], a[p].at[c], s_sem.at[p], r_sem.at[p], (flip(c), sec, ten)
                ).start()
            a[p][0] = src[0, rows_of(p)]

    def swap_turn(a, b, d, rs_a, s_sem, r_sem):
        for p in range(PARTS):
            await_bytes(a[p].at[pl.ds(1, replicas - 1)], rs_a.at[p])
            for j in outward:
                b[j, rows_of(p)] = a[p][jnp.bitwise_xor(pair, j)]
                send(b.at[j, rows_of(p)], d.at[j, rows_of(p)], s_sem.at[p], r_sem.at[p], (flip(j), sec, ten)).start()
            d[0, rows_of(p)] = a[p][pair]

    def await_part(a, p, sem):
        await_bytes(a.at[pl.ds(1, replicas - 1), rows_of(p)], sem.at[p])

    swap_start(mom_ref, mom_a, s_ma, r_ma)

    @pl.when(sec != 0)
    def _():
        swap_turn(mom_a, mom_b, mom_d, r_ma, s_mb, r_mb)

    def relay_mask(unit):
        return route_ref[jnp.maximum(sec - 1, 0), unit // chunks]

    def beside(off):
        return lax.rem(ten + off + tensors, tensors)

    def near_and_far(buf, unit, s_sem, r_sem):
        for kind, offs in ((1, (2, -2)), (0, (1, -1))):
            for off in offs:
                send(
                    buf.at[unit, ten], buf.at[unit, ten], s_sem.at[unit, kind], r_sem.at[unit, kind],
                    (rep, sec, beside(off)),
                ).start()

    def hand_on(buf, unit, s_sem, r_sem):
        await_bytes(buf.at[unit, pl.ds(0, 2)], r_sem.at[unit, 1])
        for way in (1, -1):
            block = buf.at[unit, beside(-2 * way)]
            half = block.at[pl.ds(0 if way == 1 else rows // 2, rows // 2)]
            for src, off in ((half, 2 * way), (block, way)):
                send(src, src, s_sem.at[unit, 2], r_sem.at[unit, 2], (rep, sec, beside(off))).start()

    def await_rest(buf, unit, r_sem):
        await_bytes(buf.at[unit, pl.ds(0, 2)], r_sem.at[unit, 0])
        await_bytes(buf.at[unit, pl.ds(0, 3)], r_sem.at[unit, 2])

    def stage_pick(unit):
        await_bytes(first_buf.at[unit], r_first.at[unit])
        second_buf[unit, 0] = choose([first_buf[unit, e] for e in range(n_first)], relay_mask(unit), first_bits)
        for j in range(1, n_second):
            send(
                second_buf.at[unit, 0], second_buf.at[unit, j], s_second.at[unit], r_second.at[unit],
                (flip(spread(j, second_bits)), sec, ten),
            ).start()

    def stage_gather(unit):
        @pl.when(sec == 0)
        def _():
            x_buf[unit, ten] = tok_ref[unit]

        @pl.when(sec != 0)
        def _():
            await_bytes(second_buf.at[unit, pl.ds(1, n_second - 1)], r_second.at[unit])
            x_buf[unit, ten] = choose([second_buf[unit, j] for j in range(n_second)], relay_mask(unit), second_bits)

        near_and_far(x_buf, unit, s_x, r_x)

    def stage_hand_x(unit):
        hand_on(x_buf, unit, s_x, r_x)

    def stage_hand_heads(unit):
        hand_on(heads_buf, unit, s_h, r_h)

    def stage_attend(unit):
        micro, chunk = unit // chunks, lax.rem(unit, chunks)
        anchor = rep
        for earlier in range(last):
            anchor = jnp.bitwise_xor(anchor, jnp.where(earlier < sec, route_ref[earlier, micro], 0))
        await_rest(x_buf, unit, r_x)
        width = x_buf.shape[3]
        total = jnp.zeros((rows, 3 * HD), jnp.float32)
        squares = jnp.zeros((rows, width), jnp.float32)
        for b in range(tensors):
            block = x_buf[unit, b]
            deep = pl.ds(b * width, width)
            total += jnp.dot(block, w_ref[deep, :], preferred_element_type=jnp.float32)
            wide = block.astype(jnp.float32)
            squares += wide * wide
        mean = jnp.sum(squares, axis=1, keepdims=True) * (1.0 / (width * tensors))
        qkv = (total * lax.rsqrt(mean + norm_eps)).astype(jnp.bfloat16)
        k_buf[micro, chunk] = qkv[:, HD : 2 * HD]
        v_buf[micro, chunk] = qkv[:, 2 * HD :]
        length = chunks * rows
        keys = k_buf[micro].reshape(length, HD)
        values = v_buf[micro].reshape(length, HD)
        scores = lax.dot_general(
            qkv[:, :HD], keys, (((1,), (1,)), ((), ())), preferred_element_type=jnp.float32
        ) * HD ** (-0.5)
        row_ids = lax.broadcasted_iota(jnp.int32, (rows, length), 0) + chunk * rows
        col_ids = lax.broadcasted_iota(jnp.int32, (rows, length), 1)
        here = pos_ref[anchor, pl.ds(micro, 1), :]
        doc_pos = jnp.sum(
            jnp.where(row_ids == col_ids, jnp.broadcast_to(here, (rows, length)), 0), axis=1, keepdims=True
        )
        allowed = (col_ids <= row_ids) & (row_ids - col_ids <= doc_pos)
        scores = jnp.where(allowed, scores, neg_fill)
        expo = jnp.exp(scores - jnp.max(scores, axis=1, keepdims=True))
        probability = (expo / jnp.sum(expo, axis=1, keepdims=True)).astype(jnp.bfloat16)
        heads = jnp.dot(probability, values, preferred_element_type=jnp.float32)
        heads_buf[unit, ten] = heads.astype(jnp.bfloat16)
        near_and_far(heads_buf, unit, s_h, r_h)

    def stage_out(unit):
        await_rest(heads_buf, unit, r_h)
        total = x_buf[unit, ten].astype(jnp.float32)
        for b in range(0, tensors, 2):
            both = jnp.concatenate([heads_buf[unit, b], heads_buf[unit, b + 1]], axis=1)
            total += jnp.dot(both, wo_ref[pl.ds(b * HD, 2 * HD), :], preferred_element_type=jnp.float32)
        out_ref[unit] = total.astype(jnp.bfloat16)

        @pl.when(sec != last)
        def _():
            for e in range(n_first - 1, -1, -1):
                send(
                    out_ref.at[unit], first_buf.at[unit, e], s_first.at[unit], r_first.at[unit],
                    (flip(spread(e, first_bits)), lax.rem(sec + 1, sections), ten),
                ).start()

    stages = {
        "pick": stage_pick, "gather": stage_gather, "hand_x": stage_hand_x,
        "attend": stage_attend, "hand_heads": stage_hand_heads, "out": stage_out,
    }

    piece = delta_buf.shape[1]
    per_head = HD // piece if piece <= HD else 1
    scale = inner_rate / math.sqrt(units * rows)
    early = (0, units // 2, units - max(1, units // 8))

    def add_up(start, stop, fresh, finish):
        def head(h, carry):
            count = stop - start
            mine = heads_buf[pl.ds(start, count), h].reshape(count * rows, HD)
            grad = lax.dot_general(
                mine, grad_ref[pl.ds(start * rows, count * rows), :], (((0,), (0,)), ((), ())),
                preferred_element_type=jnp.float32,
            )
            if not fresh:
                grad = grad + grad_acc[h]
            if finish:
                delta = (grad * scale).astype(jnp.bfloat16)
                for q in range(per_head):
                    delta_buf[h * per_head + q] = delta[q * piece : (q + 1) * piece]
            else:
                grad_acc[h] = grad
            return carry

        lax.fori_loop(0, tensors, head, 0)

    def pass_go():
        pl.semaphore_signal(go, inc=1, device_id=(rep, lax.rem(sec + last, sections), ten), device_id_type=MESH)

    def tick(t, carry):
        for name, late in SCHEDULE:
            unit = t - late
            due = (unit >= 0) & (unit < units)
            if name == "pick":
                due = due & (sec != 0)
            pl.when(due)(functools.partial(stages[name], unit))

        @pl.when((sec == 0) & (t == units // 2))
        def _():
            swap_turn(mom_a, mom_b, mom_d, r_ma, s_mb, r_mb)

        @pl.when((sec == last) & (t == units - 1))
        def _():
            pass_go()

        done = t - dict(SCHEDULE)['out'] + 1
        for start, stop in zip(early, early[1:]):
            pl.when((sec == last) & (done == stop))(functools.partial(add_up, start, stop, start == 0, False))
        return carry

    lax.fori_loop(0, units + max(late for _, late in SCHEDULE), tick, 0)

    @pl.when(sec == last)
    def _():
        add_up(early[-1], units, False, True)

    @pl.when(sec != last)
    def _():
        add_up(0, units, True, True)

    @pl.when(sec != last)
    def _():
        pl.semaphore_wait(go, 1)

    @pl.when((sec != last) & (sec != 0))
    def _():
        pass_go()

    swap_start(delta_buf, del_a, s_da, r_da)

    swap_turn(del_a, del_b, del_d, r_da, s_db, r_db)
    for p in range(PARTS):
        await_part(mom_d, p, r_mb)

    def update(p, c):
        span = rows_of(p)
        there = jnp.bitwise_xor(pair, c)
        mean_delta = 0.5 * (delta_buf[c, span].astype(jnp.float32) + del_d[there, span].astype(jnp.float32))
        both = mom_ref[c, span].astype(jnp.float32) + mom_d[there, span].astype(jnp.float32)
        momentum_next = outer_beta * 0.5 * both + mean_delta
        old = wo_ref[pl.ds(pl.multiple_of(c * piece + p * part, part), part), :].astype(jnp.float32)
        slow_ref[c, span] = (old - outer_rate * (outer_beta * momentum_next + mean_delta)).astype(jnp.bfloat16)
        newm_ref[c, span] = momentum_next.astype(jnp.bfloat16)

    for p in range(PARTS):
        await_part(del_d, p, r_db)

    def update_all(c, carry):
        for p in range(PARTS):
            update(p, c)
        return carry

    lax.fori_loop(0, replicas, update_all, 0)

    for p in range(PARTS):
        await_part(mom_d, p, s_ma)
    for p in range(PARTS):
        await_part(mom_d, p, s_mb)
    for p in range(PARTS):
        await_part(mom_d, p, s_da)
    for p in range(PARTS):
        await_part(mom_d, p, s_db)

    def drain(u, carry):
        for kind, blocks in ((0, 2), (1, 2), (2, 3)):
            await_bytes(x_buf.at[u, pl.ds(0, blocks)], s_x.at[u, kind])
            await_bytes(heads_buf.at[u, pl.ds(0, blocks)], s_h.at[u, kind])

        @pl.when(sec != 0)
        def _():
            await_bytes(second_buf.at[u, pl.ds(1, n_second - 1)], s_second.at[u])

        @pl.when(sec != last)
        def _():
            await_bytes(first_buf.at[u], s_first.at[u])

        return carry

    lax.fori_loop(0, units, drain, 0)


def shards(sizes, tokens, query_weight, key_weight, value_weight, slow_output, momentum, out_grad, route_keys,
           gossip_partner, positions):
    replicas, sections, tensors = sizes
    _, micros, length, width = tokens.shape
    chunks = CHUNKS
    rows = length // chunks
    units = micros * chunks
    wo = slow_output[0, 0]
    high = wo.shape[0]
    piece = high // replicas
    first_bits, second_bits = bit_groups(replicas)
    n_first, n_second = 1 << len(first_bits), 1 << len(second_bits)
    bf = jnp.bfloat16
    swap = pltpu.VMEM((replicas, piece, width), bf)
    dma = pltpu.SemaphoreType.DMA
    vmem = pl.BlockSpec(memory_space=pltpu.VMEM)
    smem = pl.BlockSpec(memory_space=pltpu.SMEM)
    hbm = pl.BlockSpec(memory_space=pl.ANY)
    cfg = (replicas, sections, tensors, units, chunks, rows)
    out, slow, newm = pl.pallas_call(
        functools.partial(kernel, cfg),
        out_shape=(
            jax.ShapeDtypeStruct((units, rows, width), bf),
            jax.ShapeDtypeStruct((replicas, piece, width), bf),
            jax.ShapeDtypeStruct((replicas, piece, width), bf),
        ),
        in_specs=[smem, smem] + [hbm] * 8,
        out_specs=(vmem, vmem, vmem),
        scratch_shapes=[
            pltpu.VMEM(positions.shape, jnp.int32),
            pltpu.VMEM((units, rows, width), bf),
            pltpu.VMEM((width * tensors, 3 * HD), bf),
            pltpu.VMEM(wo.shape, bf),
            swap,
            pltpu.VMEM((units * rows, width), bf),
            pltpu.VMEM((tensors, HD, width), jnp.float32),
            pltpu.VMEM((units, n_first, rows, width), bf),
            pltpu.VMEM((units, n_second, rows, width), bf),
            pltpu.VMEM((units, tensors, rows, width), bf),
            pltpu.VMEM((units, tensors, rows, HD), bf),
            pltpu.VMEM((micros, chunks, rows, HD), bf),
            pltpu.VMEM((micros, chunks, rows, HD), bf),
            swap, swap, swap, swap, swap,
            [pltpu.VMEM((replicas, piece // PARTS, width), bf)] * (2 * PARTS),
        ]
        + [dma((units,))] * 4
        + [dma((units, 3))] * 4
        + [dma((PARTS,))] * 8
        + [dma((8,)), pltpu.SemaphoreType.REGULAR],
        compiler_params=pltpu.CompilerParams(
            collective_id=0, has_side_effects=True, vmem_limit_bytes=52 * 1024 * 1024
        ),
    )(
        route_keys, gossip_partner, positions, tokens.reshape(units, rows, width),
        query_weight[0, 0], key_weight[0, 0], value_weight[0, 0], wo,
        momentum.reshape(replicas, piece, width), out_grad.reshape(units * rows, width),
    )
    return (
        out.reshape(1, 1, micros, length, width),
        slow.reshape(1, 1, high, width),
        newm.reshape(1, 1, high, width),
    )


def solution(mesh):
    sizes = tuple(mesh.shape[a] for a in ("replica", "section", "tensor"))
    weights = P("replica", "section", None, "tensor")
    return jax.shard_map(
        functools.partial(shards, sizes),
        mesh=mesh,
        in_specs=(
            P("replica", None, None, "tensor"),
            weights, weights, weights, weights, weights,
            P("replica", "section", None, None, "tensor"),
            P(), P(), P(),
        ),
        out_specs=(P("replica", "section", None, None, "tensor"), weights, weights),
        check_vma=False,
    )
```

```python
import functools
import math

import jax
import jax.numpy as jnp
from jax import lax
from jax.experimental import pallas as pl
from jax.experimental.pallas import tpu as pltpu
from jax.sharding import PartitionSpec as P

MESH = pl.DeviceIdType.MESH

HD = 128
CHUNKS = 8
PARTS = 2
SCHEDULE = (("pick", 0), ("hand_x", 3), ("hand_heads", 6), ("gather", 1), ("attend", 4), ("out", 7))
inner_rate = 2.0
outer_rate = 0.7
outer_beta = 0.9
neg_fill = -1e30
norm_eps = 1e-05


def bit_groups(replicas):
    bits = replicas.bit_length() - 1
    first = [0] + ([3] if bits > 3 else [])
    second = [b for b in range(bits) if b not in first]
    return first, second


def spread(index, bits):
    return sum(((index >> i) & 1) << b for i, b in enumerate(bits))


def choose(blocks, mask, bits):
    for b in bits:
        flipped = jnp.bitwise_and(jnp.right_shift(mask, b), 1) == 1
        blocks = [jnp.where(flipped, odd, even) for even, odd in zip(blocks[::2], blocks[1::2])]
    return blocks[0]


def kernel(
    cfg,
    route_ref, gossip_ref, pos_in, tok_in, wq_in, wk_in, wv_in, wo_in, mom_in, grad_in,
    out_ref, slow_ref, newm_ref,
    pos_ref, tok_ref, w_ref, wo_ref, mom_ref, grad_ref, grad_acc,
    first_buf, second_buf, x_buf, heads_buf, k_buf, v_buf,
    delta_buf, mom_b, mom_d, del_b, del_d, landed,
    s_first, r_first, s_second, r_second, s_x, r_x, s_h, r_h,
    s_ma, r_ma, s_mb, r_mb, s_da, r_da, s_db, r_db, s_in, go,
):
    replicas, sections, tensors, units, chunks, rows = cfg
    mom_a, del_a = landed[:PARTS], landed[PARTS:]
    first_bits, second_bits = bit_groups(replicas)
    n_first, n_second = 1 << len(first_bits), 1 << len(second_bits)
    rep, sec, ten = lax.axis_index("replica"), lax.axis_index("section"), lax.axis_index("tensor")
    last = sections - 1

    def flip(mask):
        return jnp.bitwise_xor(rep, mask) if mask else rep

    loads = [
        pltpu.make_async_copy(src, dst, s_in.at[i])
        for i, (src, dst) in enumerate(
            (
                (tok_in, tok_ref),
                (pos_in, pos_ref),
                (wq_in, w_ref.at[:, pl.ds(0, HD)]),
                (wk_in, w_ref.at[:, pl.ds(HD, HD)]),
                (wv_in, w_ref.at[:, pl.ds(2 * HD, HD)]),
                (wo_in, wo_ref),
                (mom_in, mom_ref),
                (grad_in, grad_ref),
            )
        )
    ]
    for load in loads:
        load.start()

    barrier = pltpu.get_barrier_semaphore()
    greeted = 0
    for mask in range(1, replicas):
        pl.semaphore_signal(barrier, inc=1, device_id=(flip(mask), sec, ten), device_id_type=MESH)
        greeted += 1
    for off in range(1, tensors):
        pl.semaphore_signal(
            barrier, inc=1, device_id=(rep, sec, lax.rem(ten + off, tensors)), device_id_type=MESH
        )
        greeted += 1
    for way in (1, sections - 1):
        for e in range(n_first):
            pl.semaphore_signal(
                barrier,
                inc=1,
                device_id=(flip(spread(e, first_bits)), lax.rem(sec + way, sections), ten),
                device_id_type=MESH,
            )
            greeted += 1

    k_buf[...] = jnp.zeros_like(k_buf)
    v_buf[...] = jnp.zeros_like(v_buf)
    for load in loads:
        load.wait()
    pl.semaphore_wait(barrier, greeted)

    def send(src, dst, s_sem, r_sem, where):
        return pltpu.make_async_remote_copy(
            src_ref=src, dst_ref=dst, send_sem=s_sem, recv_sem=r_sem, device_id=where, device_id_type=MESH
        )

    def await_bytes(ref, sem):
        pltpu.make_async_copy(ref, ref, sem).wait()

    pair = gossip_ref[sec, 0]

    part = mom_ref.shape[1] // PARTS
    outward = sorted(range(1, replicas), key=lambda c: (-(c >> 3), -((c >> 1) & 3 == 2), -(c >> 1)))

    def rows_of(p):
        return pl.ds(p * part, part)

    def swap_start(src, a, s_sem, r_sem):
        for p in range(PARTS):
            for c in outward:
                send(
                    src.at[c, rows_of(p)], a[p].at[c], s_sem.at[p], r_sem.at[p], (flip(c), sec, ten)
                ).start()
            a[p][0] = src[0, rows_of(p)]

    def swap_turn(a, b, d, rs_a, s_sem, r_sem):
        for p in range(PARTS):
            await_bytes(a[p].at[pl.ds(1, replicas - 1)], rs_a.at[p])
            for j in outward:
                b[j, rows_of(p)] = a[p][jnp.bitwise_xor(pair, j)]
                send(b.at[j, rows_of(p)], d.at[j, rows_of(p)], s_sem.at[p], r_sem.at[p], (flip(j), sec, ten)).start()
            d[0, rows_of(p)] = a[p][pair]

    def await_part(a, p, sem):
        await_bytes(a.at[pl.ds(1, replicas - 1), rows_of(p)], sem.at[p])

    swap_start(mom_ref, mom_a, s_ma, r_ma)

    @pl.when(sec != 0)
    def _():
        swap_turn(mom_a, mom_b, mom_d, r_ma, s_mb, r_mb)

    def relay_mask(unit):
        return route_ref[unit // chunks, jnp.maximum(sec - 1, 0)]

    def beside(off):
        return lax.rem(ten + off + tensors, tensors)

    def near_and_far(buf, unit, s_sem, r_sem):
        for kind, offs in ((1, (2, -2)), (0, (1, -1))):
            for off in offs:
                send(
                    buf.at[unit, ten], buf.at[unit, ten], s_sem.at[unit, kind], r_sem.at[unit, kind],
                    (rep, sec, beside(off)),
                ).start()

    def hand_on(buf, unit, s_sem, r_sem):
        await_bytes(buf.at[unit, pl.ds(0, 2)], r_sem.at[unit, 1])
        for way in (1, -1):
            block = buf.at[unit, beside(-2 * way)]
            half = block.at[pl.ds(0 if way == 1 else rows // 2, rows // 2)]
            for src, off in ((half, 2 * way), (block, way)):
                send(src, src, s_sem.at[unit, 2], r_sem.at[unit, 2], (rep, sec, beside(off))).start()

    def await_rest(buf, unit, r_sem):
        await_bytes(buf.at[unit, pl.ds(0, 2)], r_sem.at[unit, 0])
        await_bytes(buf.at[unit, pl.ds(0, 3)], r_sem.at[unit, 2])

    def stage_pick(unit):
        await_bytes(first_buf.at[unit], r_first.at[unit])
        second_buf[unit, 0] = choose([first_buf[unit, e] for e in range(n_first)], relay_mask(unit), first_bits)
        for j in range(1, n_second):
            send(
                second_buf.at[unit, 0], second_buf.at[unit, j], s_second.at[unit], r_second.at[unit],
                (flip(spread(j, second_bits)), sec, ten),
            ).start()

    def stage_gather(unit):
        @pl.when(sec == 0)
        def _():
            x_buf[unit, ten] = tok_ref[unit]

        @pl.when(sec != 0)
        def _():
            await_bytes(second_buf.at[unit, pl.ds(1, n_second - 1)], r_second.at[unit])
            x_buf[unit, ten] = choose([second_buf[unit, j] for j in range(n_second)], relay_mask(unit), second_bits)

        near_and_far(x_buf, unit, s_x, r_x)

    def stage_hand_x(unit):
        hand_on(x_buf, unit, s_x, r_x)

    def stage_hand_heads(unit):
        hand_on(heads_buf, unit, s_h, r_h)

    def stage_attend(unit):
        micro, chunk = unit // chunks, lax.rem(unit, chunks)
        anchor = rep
        for earlier in range(last):
            anchor = jnp.bitwise_xor(anchor, jnp.where(earlier < sec, route_ref[micro, earlier], 0))
        await_rest(x_buf, unit, r_x)
        width = x_buf.shape[3]
        total = jnp.zeros((rows, 3 * HD), jnp.float32)
        squares = jnp.zeros((rows, width), jnp.float32)
        for b in range(tensors):
            block = x_buf[unit, b]
            deep = pl.ds(b * width, width)
            total += jnp.dot(block, w_ref[deep, :], preferred_element_type=jnp.float32)
            wide = block.astype(jnp.float32)
            squares += wide * wide
        mean = jnp.sum(squares, axis=1, keepdims=True) * (1.0 / (width * tensors))
        qkv = (total * lax.rsqrt(mean + norm_eps)).astype(jnp.bfloat16)
        k_buf[micro, chunk] = qkv[:, HD : 2 * HD]
        v_buf[micro, chunk] = qkv[:, 2 * HD :]
        length = chunks * rows
        keys = k_buf[micro].reshape(length, HD)
        values = v_buf[micro].reshape(length, HD)
        scores = lax.dot_general(
            qkv[:, :HD], keys, (((1,), (1,)), ((), ())), preferred_element_type=jnp.float32
        ) * HD ** (-0.5)
        row_ids = lax.broadcasted_iota(jnp.int32, (rows, length), 0) + chunk * rows
        col_ids = lax.broadcasted_iota(jnp.int32, (rows, length), 1)
        here = pos_ref[anchor, pl.ds(micro, 1), :]
        doc_pos = jnp.sum(
            jnp.where(row_ids == col_ids, jnp.broadcast_to(here, (rows, length)), 0), axis=1, keepdims=True
        )
        allowed = (col_ids <= row_ids) & (row_ids - col_ids <= doc_pos)
        scores = jnp.where(allowed, scores, neg_fill)
        expo = jnp.exp(scores - jnp.max(scores, axis=1, keepdims=True))
        probability = (expo / jnp.sum(expo, axis=1, keepdims=True)).astype(jnp.bfloat16)
        heads = jnp.dot(probability, values, preferred_element_type=jnp.float32)
        heads_buf[unit, ten] = heads.astype(jnp.bfloat16)
        near_and_far(heads_buf, unit, s_h, r_h)

    def stage_out(unit):
        await_rest(heads_buf, unit, r_h)
        total = x_buf[unit, ten].astype(jnp.float32)
        for b in range(0, tensors, 2):
            both = jnp.concatenate([heads_buf[unit, b], heads_buf[unit, b + 1]], axis=1)
            total += jnp.dot(both, wo_ref[pl.ds(b * HD, 2 * HD), :], preferred_element_type=jnp.float32)
        out_ref[unit] = total.astype(jnp.bfloat16)

        @pl.when(sec != last)
        def _():
            for e in range(n_first - 1, -1, -1):
                send(
                    out_ref.at[unit], first_buf.at[unit, e], s_first.at[unit], r_first.at[unit],
                    (flip(spread(e, first_bits)), lax.rem(sec + 1, sections), ten),
                ).start()

    stages = {
        "pick": stage_pick, "gather": stage_gather, "hand_x": stage_hand_x,
        "attend": stage_attend, "hand_heads": stage_hand_heads, "out": stage_out,
    }

    piece = delta_buf.shape[1]
    per_head = HD // piece if piece <= HD else 1
    scale = inner_rate / math.sqrt(units * rows)
    early = (0, units // 2, units - max(1, units // 8))

    def add_up(start, stop, fresh, finish):
        def head(h, carry):
            count = stop - start
            mine = heads_buf[pl.ds(start, count), h].reshape(count * rows, HD)
            grad = lax.dot_general(
                mine, grad_ref[pl.ds(start * rows, count * rows), :], (((0,), (0,)), ((), ())),
                preferred_element_type=jnp.float32,
            )
            if not fresh:
                grad = grad + grad_acc[h]
            if finish:
                delta = (grad * scale).astype(jnp.bfloat16)
                for q in range(per_head):
                    delta_buf[h * per_head + q] = delta[q * piece : (q + 1) * piece]
            else:
                grad_acc[h] = grad
            return carry

        lax.fori_loop(0, tensors, head, 0)

    def pass_go():
        pl.semaphore_signal(go, inc=1, device_id=(rep, lax.rem(sec + last, sections), ten), device_id_type=MESH)

    def tick(t, carry):
        for name, late in SCHEDULE:
            unit = t - late
            due = (unit >= 0) & (unit < units)
            if name == "pick":
                due = due & (sec != 0)
            pl.when(due)(functools.partial(stages[name], unit))

        @pl.when((sec == 0) & (t == units // 2))
        def _():
            swap_turn(mom_a, mom_b, mom_d, r_ma, s_mb, r_mb)

        @pl.when((sec == last) & (t == units - 2))
        def _():
            pass_go()

        done = t - dict(SCHEDULE)['out'] + 1
        for start, stop in zip(early, early[1:]):
            pl.when((sec == last) & (done == stop))(functools.partial(add_up, start, stop, start == 0, False))
        return carry

    lax.fori_loop(0, units + max(late for _, late in SCHEDULE), tick, 0)

    @pl.when(sec == last)
    def _():
        add_up(early[-1], units, False, True)

    @pl.when(sec != last)
    def _():
        add_up(0, units, True, True)

    @pl.when(sec != last)
    def _():
        pl.semaphore_wait(go, 1)

    @pl.when((sec != last) & (sec != 0))
    def _():
        pass_go()

    swap_start(delta_buf, del_a, s_da, r_da)

    swap_turn(del_a, del_b, del_d, r_da, s_db, r_db)
    for p in range(PARTS):
        await_part(mom_d, p, r_mb)

    def update(p, c):
        span = rows_of(p)
        there = jnp.bitwise_xor(pair, c)
        mean_delta = 0.5 * (delta_buf[c, span].astype(jnp.float32) + del_d[there, span].astype(jnp.float32))
        both = mom_ref[c, span].astype(jnp.float32) + mom_d[there, span].astype(jnp.float32)
        momentum_next = outer_beta * 0.5 * both + mean_delta
        old = wo_ref[pl.ds(pl.multiple_of(c * piece + p * part, part), part), :].astype(jnp.float32)
        slow_ref[c, span] = (old - outer_rate * (outer_beta * momentum_next + mean_delta)).astype(jnp.bfloat16)
        newm_ref[c, span] = momentum_next.astype(jnp.bfloat16)

    for p in range(PARTS):
        await_part(del_d, p, r_db)

    def update_all(c, carry):
        for p in range(PARTS):
            update(p, c)
        return carry

    lax.fori_loop(0, replicas, update_all, 0)

    for p in range(PARTS):
        await_part(mom_d, p, s_ma)
    for p in range(PARTS):
        await_part(mom_d, p, s_mb)
    for p in range(PARTS):
        await_part(mom_d, p, s_da)
    for p in range(PARTS):
        await_part(mom_d, p, s_db)

    def drain(u, carry):
        for kind, blocks in ((0, 2), (1, 2), (2, 3)):
            await_bytes(x_buf.at[u, pl.ds(0, blocks)], s_x.at[u, kind])
            await_bytes(heads_buf.at[u, pl.ds(0, blocks)], s_h.at[u, kind])

        @pl.when(sec != 0)
        def _():
            await_bytes(second_buf.at[u, pl.ds(1, n_second - 1)], s_second.at[u])

        @pl.when(sec != last)
        def _():
            await_bytes(first_buf.at[u], s_first.at[u])

        return carry

    lax.fori_loop(0, units, drain, 0)


def shards(sizes, tokens, query_weight, key_weight, value_weight, slow_output, momentum, out_grad, route_keys,
           gossip_partner, positions):
    replicas, sections, tensors = sizes
    _, micros, length, width = tokens.shape
    chunks = CHUNKS
    rows = length // chunks
    units = micros * chunks
    wo = slow_output[0, 0]
    high = wo.shape[0]
    piece = high // replicas
    first_bits, second_bits = bit_groups(replicas)
    n_first, n_second = 1 << len(first_bits), 1 << len(second_bits)
    bf = jnp.bfloat16
    swap = pltpu.VMEM((replicas, piece, width), bf)
    dma = pltpu.SemaphoreType.DMA
    vmem = pl.BlockSpec(memory_space=pltpu.VMEM)
    smem = pl.BlockSpec(memory_space=pltpu.SMEM)
    hbm = pl.BlockSpec(memory_space=pl.ANY)
    cfg = (replicas, sections, tensors, units, chunks, rows)
    out, slow, newm = pl.pallas_call(
        functools.partial(kernel, cfg),
        out_shape=(
            jax.ShapeDtypeStruct((units, rows, width), bf),
            jax.ShapeDtypeStruct((replicas, piece, width), bf),
            jax.ShapeDtypeStruct((replicas, piece, width), bf),
        ),
        in_specs=[smem, smem] + [hbm] * 8,
        out_specs=(vmem, vmem, vmem),
        scratch_shapes=[
            pltpu.VMEM(positions.shape, jnp.int32),
            pltpu.VMEM((units, rows, width), bf),
            pltpu.VMEM((width * tensors, 3 * HD), bf),
            pltpu.VMEM(wo.shape, bf),
            swap,
            pltpu.VMEM((units * rows, width), bf),
            pltpu.VMEM((tensors, HD, width), jnp.float32),
            pltpu.VMEM((units, n_first, rows, width), bf),
            pltpu.VMEM((units, n_second, rows, width), bf),
            pltpu.VMEM((units, tensors, rows, width), bf),
            pltpu.VMEM((units, tensors, rows, HD), bf),
            pltpu.VMEM((micros, chunks, rows, HD), bf),
            pltpu.VMEM((micros, chunks, rows, HD), bf),
            swap, swap, swap, swap, swap,
            [pltpu.VMEM((replicas, piece // PARTS, width), bf)] * (2 * PARTS),
        ]
        + [dma((units,))] * 4
        + [dma((units, 3))] * 4
        + [dma((PARTS,))] * 8
        + [dma((8,)), pltpu.SemaphoreType.REGULAR],
        compiler_params=pltpu.CompilerParams(
            collective_id=0, has_side_effects=True, vmem_limit_bytes=52 * 1024 * 1024
        ),
    )(
        route_keys.T, gossip_partner, positions, tokens.reshape(units, rows, width),
        query_weight[0, 0], key_weight[0, 0], value_weight[0, 0], wo,
        momentum.reshape(replicas, piece, width), out_grad.reshape(units * rows, width),
    )
    return (
        out.reshape(1, 1, micros, length, width),
        slow.reshape(1, 1, high, width),
        newm.reshape(1, 1, high, width),
    )


def solution(mesh):
    sizes = tuple(mesh.shape[a] for a in ("replica", "section", "tensor"))
    weights = P("replica", "section", None, "tensor")
    return jax.shard_map(
        functools.partial(shards, sizes),
        mesh=mesh,
        in_specs=(
            P("replica", None, None, "tensor"),
            weights, weights, weights, weights, weights,
            P("replica", "section", None, None, "tensor"),
            P(), P(), P(),
        ),
        out_specs=(P("replica", "section", None, None, "tensor"), weights, weights),
        check_vma=False,
    )
```
